256 devices in a mesh: tm: 8 (over y, core), chan: 32 (over x, z).
Axes of the slice: x: 4, y: 4, z: 8, core: 2. Of those that a mesh axis runs over, the one named last changes fastest.
Arguments:
- records: bfloat16 [24, 5120, 3000], P('tm', 'chan'), may hold values from -6 to 6
- partner: int32 [32, 7], P('chan'), may hold values from 0 to 31, as said below
- valid: int32 [32, 7], P('chan'), may hold values from 0 to 1
Outputs:
- stacked: bfloat16 [2, 32, 35840, 160], P(None, 'tm', 'chan')
The draws below stay inside these ranges and needn't reach their ends.
Inputs may be any that keep to these rules, and one draw needn't show every extreme that they name: Each partner lies within 3 of its row's block index; the valid partners of a row are distinct, and padded slots name the row's own block.
All inputs are finite; a program needn't handle non-finite values.
Results may differ from the reference program's by a relative error of at most 0.0066.
Values may be sent and summed in bfloat16 or wider, within the bound.
No kernel may reach another device: no remote copies, remote signals or barrier semaphores. Data moves between devices by JAX's collectives and lax.ppermute only.
A program may use at most 64 MiB of HBM per device.

```python
import math
import jax
import jax.numpy as jnp
from jax import lax

CB = 160
SAMPLES = 3000
BINS = 32
REACH = 3
PAIRS = 7
BLOCKS = 32
CHANNELS = 5120
SEG = 24


def tile_lists(key):
    offsets = jnp.arange(PAIRS, dtype=jnp.int32) - REACH
    row_keys = jax.random.split(jax.random.fold_in(key, 11), BLOCKS)
    shuffled = jax.vmap(lambda k: jax.random.permutation(k, offsets))(row_keys)
    blocks = jnp.arange(BLOCKS, dtype=jnp.int32)[:, None]
    target = blocks + shuffled
    inside = (target >= 0) & (target < BLOCKS)
    keep = jax.random.randint(jax.random.fold_in(key, 12), (BLOCKS, PAIRS), 0, 4) > 0
    chosen = inside & (keep | (shuffled == 0))
    partner_out = jnp.where(chosen, target, blocks).astype(jnp.int32)
    return (partner_out, chosen.astype(jnp.int32))


def draw_partner(key, part):
    partner_out, chosen = tile_lists(key)
    return partner_out


def draw_valid(key, part):
    partner_out, chosen = tile_lists(key)
    return chosen


def shard_levels(own_key, shape, shards, smallest, high):
    factor_of, own = 1.0, jax.random.fold_in(own_key, 6)
    for axis_at, parts in shards:
        heights = jnp.exp(jax.random.uniform(jax.random.fold_in(own, axis_at), (parts,), jnp.float32, smallest / len(shards), high / len(shards)))
        factor_of = factor_of * jnp.repeat(heights, shape[axis_at] // parts).reshape([-1 if axis == axis_at else 1 for axis in range(len(shape))])
    return factor_of


def centred(own_key, dims, spread, bound, cuts=(), kind=jnp.bfloat16):
    entries = spread * jax.random.normal(own_key, dims, jnp.float32)
    if cuts:
        entries = entries * shard_levels(own_key, dims, cuts, -0.22, 0.18)
    return jnp.clip(entries, -bound, bound).astype(kind)


def setup_inputs(seed: int = 0) -> dict:
    keys = jax.random.split(jax.random.key(seed), 4)
    return {
        "records": centred(keys[0], (SEG, CHANNELS, SAMPLES), 1.0, 6.0, ((0, 8), (1, 32))),
        "partner": draw_partner(jax.random.fold_in(keys[3], 71), 0),
        "valid": draw_valid(jax.random.fold_in(keys[3], 71), 0),
    }


def spectra_table(length, bins):
    times = lax.iota(jnp.int32, length)
    freqs = 60 + 10 * lax.iota(jnp.int32, bins)
    phase = freqs[:, None] * times[None, :] % length
    angle = phase.astype(jnp.float32) * (2.0 * math.pi / length)
    return jnp.concatenate([jnp.cos(angle), -jnp.sin(angle)], 0).astype(jnp.bfloat16)

def reference(records, partner, valid):
    table = spectra_table(SAMPLES, BINS).astype(jnp.float32)

    def one_segment(record):
        spectrum = jnp.einsum('kl,cl->kc', table, record.astype(jnp.float32))
        power = lax.optimization_barrier(jnp.mean(spectrum * spectrum, axis=0, keepdims=True))
        return (spectrum * lax.rsqrt(power + 1e-06)).astype(jnp.bfloat16)
    white = lax.map(one_segment, records).reshape(SEG, 2, BINS, CHANNELS)
    scale = 1.0 / math.sqrt(SEG)

    def one_block(index):
        first = lax.dynamic_slice_in_dim(white, (index * CB).astype(jnp.int32), CB, 3).astype(jnp.float32)

        def one_slot(slot):
            other = lax.dynamic_slice_in_dim(white, (partner[index, slot] * CB).astype(jnp.int32), CB, 3).astype(jnp.float32)
            real_part = jnp.einsum('sfa,sfb->fab', first[:, 0], other[:, 0]) + jnp.einsum('sfa,sfb->fab', first[:, 1], other[:, 1])
            imag_part = jnp.einsum('sfa,sfb->fab', first[:, 1], other[:, 0]) - jnp.einsum('sfa,sfb->fab', first[:, 0], other[:, 1])
            weight = valid[index, slot].astype(jnp.float32) * scale
            return (jnp.stack([real_part, imag_part], 0) * weight).astype(jnp.bfloat16)
        return lax.map(one_slot, jnp.arange(PAIRS, dtype=jnp.int32))
    tiles = lax.map(one_block, jnp.arange(BLOCKS, dtype=jnp.int32))
    tiles = jnp.transpose(tiles, (2, 3, 0, 1, 4, 5))
    return tiles.reshape(2, BINS, BLOCKS * PAIRS * CB, CB)
```

```python
import functools
import math

import jax
import jax.numpy as jnp
import numpy as np
from jax import lax
from jax.experimental import pallas as pl
from jax.experimental.pallas import tpu as pltpu
from jax.sharding import Mesh
from jax.sharding import PartitionSpec as P

BINS = 32
REACH = 3
SLOTS = 7
WIDTH = 160
LANES = 128
TAIL = WIDTH - LANES
TM = 8
SEG_LOCAL = 3
LOCAL_BINS = BINS // TM
ROWS = 32
DEPTH = 64
USED = 2 * SEG_LOCAL * TM
SPAN = 4 * WIDTH


def spectra_table(length):
    times = np.arange(length, dtype=np.int64)
    freqs = 60 + 10 * np.arange(BINS, dtype=np.int64)
    phase = (freqs[:, None] * times[None, :]) % length
    angle = phase.astype(np.float32) * np.float32(2.0 * math.pi / length)
    both = np.stack([np.cos(angle), -np.sin(angle)], 0)
    both = both.reshape(2, TM, LOCAL_BINS, length).transpose(1, 0, 2, 3)
    return both.reshape(2 * BINS, length).astype(jnp.bfloat16)


def source_row(seg, part, bin_, owner):
    return owner * ROWS + (8 * SEG_LOCAL if seg is None else 8 * seg) + part * LOCAL_BINS + bin_


def depth_rows():
    rows = [(s, t, r) for s in range(SEG_LOCAL) for t in range(TM) for r in range(2)]
    return rows + [(None, t, r) for t in range(TM) for r in range(2)]


def gather_tables():
    rows = depth_rows()
    other = np.zeros((2, TM * ROWS, LOCAL_BINS * DEPTH), np.float32)
    own = np.zeros((LOCAL_BINS, 2, DEPTH, TM * ROWS), np.float32)
    for f in range(LOCAL_BINS):
        for k, (s, t, r) in enumerate(rows):
            other[0, source_row(s, r, f, t), f * DEPTH + k] = 1
            other[1, source_row(s, r, f, t), (f ^ 1) * DEPTH + k] = 1
            own[f, 0, k, source_row(s, r, f, t)] = 1
            own[f, 1, k, source_row(s, 1 - r, f, t)] = 1 if r == 0 else -1
    return other.astype(jnp.bfloat16), own.reshape(LOCAL_BINS, 2 * DEPTH, -1).astype(jnp.bfloat16)


def whiten_kernel(table_ref, records_ref, out_ref, tail_ref):
    s = pl.program_id(0)
    spectrum = lax.dot_general(
        table_ref[...],
        records_ref[0],
        (((1,), (1,)), ((), ())),
        preferred_element_type=jnp.float32,
    )
    power = jnp.mean(spectrum * spectrum, axis=0, keepdims=True)
    white = spectrum * lax.rsqrt(power + 1e-06)
    main = white[:, :LANES].astype(jnp.bfloat16).reshape(TM, 8, LANES)
    last = jnp.pad(white[:, LANES:], ((0, 0), (0, LANES - TAIL)))
    for step in range(SEG_LOCAL):

        @pl.when(s == step)
        def _():
            for copy in range(2):
                out_ref[:, copy, 8 * step : 8 * step + 8, :] = main
            if step == 0:
                tail_ref[...] = last
            else:
                tail_ref[...] += pltpu.roll(last, TAIL * step, 1)
            if step == SEG_LOCAL - 1:
                tails = tail_ref[...].astype(jnp.bfloat16).reshape(TM, 8, LANES)
                for copy in range(2):
                    out_ref[:, copy, 8 * SEG_LOCAL :, :] = tails


def whiten(records, table):
    length = records.shape[2]
    return pl.pallas_call(
        whiten_kernel,
        grid=(SEG_LOCAL,),
        in_specs=[
            pl.BlockSpec((2 * BINS, length), lambda s: (0, 0)),
            pl.BlockSpec((1, WIDTH, length), lambda s: (s, 0, 0)),
        ],
        out_specs=pl.BlockSpec((TM, 2, ROWS, LANES), lambda s: (0, 0, 0, 0)),
        out_shape=jax.ShapeDtypeStruct((TM, 2, ROWS, LANES), jnp.bfloat16),
        scratch_shapes=[pltpu.VMEM((2 * BINS, LANES), jnp.float32)],
        compiler_params=pltpu.CompilerParams(vmem_limit_bytes=32 << 20),
    )(table, records)


def stack_kernel(
    offset_ref, valid_ref, odd_ref, mine_ref, near_ref, far_ref, edge_ref, gather_ref, own_ref,
    out_ref, left_ref, block_ref,
):
    f = pl.program_id(0)
    odd = odd_ref[0]

    @pl.when(f == 0)
    def _():
        for i in range(2):
            block_ref[i] = near_ref[:, i].reshape(TM * ROWS, LANES)
            block_ref[2 + i] = mine_ref[:, i].reshape(TM * ROWS, LANES)
            block_ref[4 + i] = far_ref[:, i].reshape(TM * ROWS, LANES)
        block_ref[6] = edge_ref[...].reshape(TM * ROWS, LANES)
        lane = lax.broadcasted_iota(jnp.int32, (TAIL, 4 * DEPTH), 1) % DEPTH
        halves = [None, None]
        for p in range(8):
            if p < SLOTS:
                d = offset_ref[0, p]
                at_even = jnp.where(d == -3, 6, d + 2)
                at_odd = jnp.where(
                    d == 3, 6, jnp.where(d <= -2, d + 7, jnp.where(d <= 0, d + 3, d - 1))
                )
                block = block_ref[jnp.where(odd == 1, at_odd, at_even)]
                turned = lax.dot_general(
                    block,
                    gather_ref[p % 2],
                    (((0,), (0,)), ((), ())),
                    preferred_element_type=jnp.float32,
                )
                last = jnp.zeros((TAIL, 4 * DEPTH), jnp.float32)
                for s in range(SEG_LOCAL):
                    moved = pltpu.roll(
                        turned[TAIL * s : TAIL * (s + 1)], (16 * s - USED) % (4 * DEPTH), 1
                    )
                    last = jnp.where((lane >= 16 * s) & (lane < 16 * s + 16), moved, last)
                halves[p % 2] = jnp.concatenate([turned, last], 0)
            else:
                halves[p % 2] = jnp.zeros((WIDTH, 4 * DEPTH), jnp.float32)
            if p % 2 == 1:
                low = lax.broadcasted_iota(jnp.int32, (WIDTH, LANES), 1) < DEPTH
                for g in range(LOCAL_BINS):
                    tile = slice(LANES * (g // 2), LANES * (g // 2 + 1))
                    first, second = halves if g % 2 == 0 else halves[::-1]
                    pair = jnp.where(low, first[:, tile], second[:, tile])
                    left_ref[
                        g,
                        WIDTH * (p // 4) : WIDTH * (p // 4 + 1),
                        LANES * (p % 4 // 2) : LANES * (p % 4 // 2 + 1),
                    ] = pair.astype(jnp.bfloat16)

    own = jnp.where(odd == 1, mine_ref[:, 1], mine_ref[:, 0]).reshape(TM * ROWS, LANES)
    ordered = jnp.dot(own_ref[0], own, preferred_element_type=jnp.float32)
    lane = lax.broadcasted_iota(jnp.int32, (USED, LANES), 1)
    zero = jnp.zeros((DEPTH, LANES), jnp.bfloat16)
    fill = jnp.zeros((DEPTH - USED, LANES), jnp.bfloat16)
    column = lax.broadcasted_iota(jnp.int32, (1, 2 * SPAN), 1)
    weight = jnp.zeros((1, 2 * SPAN), jnp.float32)
    for p in range(SLOTS):
        here = (column >= WIDTH * p) & (column < WIDTH * (p + 1))
        weight = jnp.where(here, valid_ref[0, p].astype(jnp.float32), weight)
    weight = weight * (1.0 / math.sqrt(SEG_LOCAL * TM))
    for part in range(2):
        rows = ordered[DEPTH * part : DEPTH * (part + 1)]
        main, last = rows[:USED], rows[USED:]
        turns = [last if m == 0 else pltpu.roll(last, TAIL * m, 1) for m in range(4)]
        tiles = []
        for j in range(4):
            moved = main if j == 0 else pltpu.roll(main, TAIL * j, 1)
            ends = jnp.concatenate([turns[(j - s) % 4] for s in range(SEG_LOCAL)], 0)
            low = jnp.where(lane >= TAIL * j, moved, 0.0)
            high = jnp.where(
                lane < TAIL * j, moved, jnp.where(lane < TAIL * (j + 1), ends, 0.0)
            )
            tiles.append(
                [jnp.concatenate([x.astype(jnp.bfloat16), fill], 0) for x in (low, high)]
            )
        grid_rows = [
            jnp.concatenate(
                [tiles[j][c - j] if 0 <= c - j < 2 else zero for c in range(5)], 1
            )
            for j in range(4)
        ]
        swapped = [grid_rows[j] for j in (1, 0, 3, 2)]
        even = jnp.concatenate(grid_rows, 0)
        odd_f = jnp.concatenate(swapped, 0)
        right = jnp.where(f % 2 == 0, even, odd_f)
        product = jnp.dot(left_ref[f], right, preferred_element_type=jnp.float32)
        out_ref[part, 0, :, :SPAN] = (product[:WIDTH] * weight[:, :SPAN]).astype(jnp.bfloat16)
        out_ref[part, 0, :, SPAN:] = (
            product[WIDTH:, : SLOTS * WIDTH - SPAN] * weight[:, SPAN : SLOTS * WIDTH]
        ).astype(jnp.bfloat16)


def stack(offsets, valid, odd, mine, near, far, edge, gather, own):
    whole = lambda *shape: pl.BlockSpec(shape, lambda f: (0,) * len(shape))
    scalars = pl.BlockSpec(memory_space=pltpu.SMEM)
    return pl.pallas_call(
        stack_kernel,
        grid=(LOCAL_BINS,),
        in_specs=[
            scalars,
            scalars,
            scalars,
            whole(TM, 2, ROWS, LANES),
            whole(TM, 2, ROWS, LANES),
            whole(TM, 2, ROWS, LANES),
            whole(TM, ROWS, LANES),
            whole(2, TM * ROWS, LOCAL_BINS * DEPTH),
            pl.BlockSpec((1, 2 * DEPTH, TM * ROWS), lambda f: (f, 0, 0)),
        ],
        out_specs=pl.BlockSpec((2, 1, WIDTH, SLOTS * WIDTH), lambda f: (0, f, 0, 0)),
        out_shape=jax.ShapeDtypeStruct((2, LOCAL_BINS, WIDTH, SLOTS * WIDTH), jnp.bfloat16),
        scratch_shapes=[
            pltpu.VMEM((LOCAL_BINS, 2 * WIDTH, 4 * DEPTH), jnp.bfloat16),
            pltpu.VMEM((SLOTS, TM * ROWS, LANES), jnp.bfloat16),
        ],
        compiler_params=pltpu.CompilerParams(vmem_limit_bytes=32 << 20),
    )(offsets, valid, odd, mine, near, far, edge, gather, own)


def per_device(records, partner, valid):
    blocks = lax.axis_size("pair") * 2
    chan = ("pair", "side")
    side = lax.axis_index("side")
    table = jnp.asarray(spectra_table(records.shape[2]))
    gather, own = (jnp.asarray(x) for x in gather_tables())

    def fetch(array, even, odd):
        route = [((c + (odd if c % 2 else even)) % blocks, c) for c in range(blocks)]
        return lax.ppermute(array, chan, route)

    white = whiten(records, table)
    mine = lax.all_to_all(
        white.reshape(2 * TM, ROWS, LANES), ("tm", "side"), 0, 0, tiled=True
    ).reshape(TM, 2, ROWS, LANES)
    near = fetch(mine, -1, 1)
    far = fetch(mine, 2, -2)
    edge = fetch(lax.dynamic_index_in_dim(far, side, 1, keepdims=False), -1, 1)
    offsets = partner - (lax.axis_index("pair") * 2 + side)
    result = stack(offsets, valid, side.reshape(1), mine, near, far, edge, gather, own)
    return jnp.transpose(result, (0, 1, 3, 2))


def solution(mesh):
    tm, chan = mesh.shape["tm"], mesh.shape["chan"]
    paired = Mesh(mesh.devices.reshape(tm, chan // 2, 2), ("tm", "pair", "side"))
    blocks = ("pair", "side")
    return jax.shard_map(
        per_device,
        mesh=paired,
        in_specs=(P("tm", blocks, None), P(blocks, None), P(blocks, None)),
        out_specs=P(None, "tm", blocks, None),
        check_vma=False,
    )
```

```python
import functools
import math

import jax
import jax.numpy as jnp
import numpy as np
from jax import lax
from jax.experimental import pallas as pl
from jax.experimental.pallas import tpu as pltpu
from jax.sharding import Mesh
from jax.sharding import PartitionSpec as P

BINS = 32
REACH = 3
SLOTS = 7
WIDTH = 160
LANES = 128
TAIL = WIDTH - LANES
TM = 8
SEG_LOCAL = 3
LOCAL_BINS = BINS // TM
ROWS = 32
DEPTH = 64
USED = 2 * SEG_LOCAL * TM
SPAN = 4 * WIDTH
CHUNK = 512
SCOPE = 32 << 20
SPARE = 7
WHOLE = 56_000_000


def spectra_table(length):
    times = np.arange(length, dtype=np.int64)
    freqs = 60 + 10 * np.arange(BINS, dtype=np.int64)
    phase = (freqs[:, None] * times[None, :]) % length
    angle = phase.astype(np.float32) * np.float32(2.0 * math.pi / length)
    both = np.stack([np.cos(angle), -np.sin(angle)], 0)
    both = both.reshape(2, TM, LOCAL_BINS, length).transpose(1, 0, 2, 3)
    table = both.reshape(1, 2 * BINS, length).astype(jnp.bfloat16)
    return np.concatenate([table, np.zeros((SPARE, 2 * BINS, length), table.dtype)], 0)


def source_row(seg, part, bin_, owner):
    return owner * ROWS + (8 * SEG_LOCAL if seg is None else 8 * seg) + part * LOCAL_BINS + bin_


def depth_rows():
    rows = [(s, t, r) for s in range(SEG_LOCAL) for t in range(TM) for r in range(2)]
    return rows + [(None, t, r) for t in range(TM) for r in range(2)]


def gather_tables():
    rows = depth_rows()
    other = np.zeros((2, TM * ROWS, LOCAL_BINS * LANES), np.float32)
    own = np.zeros((LOCAL_BINS, 2, DEPTH, TM * ROWS), np.float32)
    for f in range(LOCAL_BINS):
        for k, (s, t, r) in enumerate(rows):
            for order in range(2):
                other[order, source_row(s, r, f, t), f * LANES + order * DEPTH + k] = 1
            own[f, 0, k, source_row(s, r, f, t)] = 1
            own[f, 1, k, source_row(s, 1 - r, f, t)] = 1 if r == 0 else -1
    return other.astype(jnp.bfloat16), own.reshape(LOCAL_BINS, 2 * DEPTH, -1).astype(jnp.bfloat16)


def whiten_kernel(table_hbm, records_hbm, out_ref, table_ref, records_ref, sems):
    length = records_ref.shape[2]
    edges = list(range(0, length, CHUNK)) + [length]
    cuts = [slice(a, b) for a, b in zip(edges[:-1], edges[1:])]
    copies = []
    for i, cut in enumerate(cuts):
        part = pl.ds(cut.start, cut.stop - cut.start)
        if i == 0:
            copies.append(pltpu.make_async_copy(table_hbm.at[0], table_ref, sems.at[len(cuts)]))
        copies.append(
            pltpu.make_async_copy(
                records_hbm.at[:, :, part], records_ref.at[:, :, part], sems.at[i]
            )
        )
    for copy in copies:
        copy.start()
    copies[0].wait()
    total = None
    for i, cut in enumerate(cuts):
        copies[i + 1].wait()
        product = lax.dot_general(
            table_ref[:, cut],
            records_ref[:, :, cut].reshape(SEG_LOCAL * WIDTH, cut.stop - cut.start),
            (((1,), (1,)), ((), ())),
            preferred_element_type=jnp.float32,
        )
        total = product if total is None else total + product
    tails = None
    for s in range(SEG_LOCAL):
        spectrum = total[:, WIDTH * s : WIDTH * (s + 1)]
        power = jnp.mean(spectrum * spectrum, axis=0, keepdims=True)
        white = spectrum * lax.rsqrt(power + 1e-06)
        main = white[:, :LANES].astype(jnp.bfloat16).reshape(TM, 8, LANES)
        last = jnp.pad(white[:, LANES:], ((0, 0), (0, LANES - TAIL)))
        tails = last if s == 0 else tails + pltpu.roll(last, TAIL * s, 1)
        for copy in range(2):
            out_ref[:, copy, 8 * s : 8 * s + 8, :] = main
    tails = tails.astype(jnp.bfloat16).reshape(TM, 8, LANES)
    for copy in range(2):
        out_ref[:, copy, 8 * SEG_LOCAL :, :] = tails


def whiten(records, table):
    cuts = -(-records.shape[2] // CHUNK)
    return pl.pallas_call(
        whiten_kernel,
        in_specs=[pl.BlockSpec(memory_space=pltpu.HBM)] * 2,
        out_specs=pl.BlockSpec(memory_space=pltpu.VMEM),
        out_shape=jax.ShapeDtypeStruct((TM, 2, ROWS, LANES), jnp.bfloat16),
        scratch_shapes=[
            pltpu.VMEM(table.shape[1:], jnp.bfloat16),
            pltpu.VMEM(records.shape, jnp.bfloat16),
            pltpu.SemaphoreType.DMA((cuts + 1,)),
        ],
        compiler_params=pltpu.CompilerParams(vmem_limit_bytes=WHOLE),
    )(table, records)


def spread_kernel(odd_ref, mine_ref, own_ref, out_ref):
    own = jnp.where(odd_ref[0] == 1, mine_ref[:, 1], mine_ref[:, 0]).reshape(TM * ROWS, LANES)
    lane = lax.broadcasted_iota(jnp.int32, (USED, LANES), 1)
    fill = jnp.zeros((DEPTH - USED, LANES), jnp.bfloat16)
    for f in range(LOCAL_BINS):
        ordered = jnp.dot(own_ref[f], own, preferred_element_type=jnp.float32)
        for part in range(2):
            rows = ordered[DEPTH * part : DEPTH * (part + 1)]
            main, last = rows[:USED], rows[USED:]
            turns = [last if m == 0 else pltpu.roll(last, TAIL * m, 1) for m in range(4)]
            for j in range(4):
                moved = main if j == 0 else pltpu.roll(main, TAIL * j, 1)
                ends = jnp.concatenate([turns[(j - s) % 4] for s in range(SEG_LOCAL)], 0)
                low = jnp.where(lane >= TAIL * j, moved, 0.0)
                high = jnp.where(
                    lane < TAIL * j, moved, jnp.where(lane < TAIL * (j + 1), ends, 0.0)
                )
                for half, x in enumerate((low, high)):
                    tile = slice(LANES * half, LANES * (half + 1))
                    out_ref[f, part, j, :USED, tile] = x.astype(jnp.bfloat16)
                    out_ref[f, part, j, USED:, tile] = fill


def spread(odd, mine, own):
    shape = (LOCAL_BINS, 2, 4, DEPTH, 2 * LANES)
    return pl.pallas_call(
        spread_kernel,
        in_specs=[pl.BlockSpec(memory_space=pltpu.SMEM)]
        + [pl.BlockSpec(memory_space=pltpu.VMEM)] * 2,
        out_specs=pl.BlockSpec(memory_space=pltpu.VMEM),
        out_shape=jax.ShapeDtypeStruct(shape, jnp.bfloat16),
        compiler_params=pltpu.CompilerParams(vmem_limit_bytes=SCOPE),
        cost_estimate=pl.CostEstimate(flops=70_000_000, bytes_accessed=3_000_000, transcendentals=0),
    )(odd, mine, own)


def turned(block, gather):
    lane = lax.broadcasted_iota(jnp.int32, (TAIL, LOCAL_BINS * LANES), 1) % DEPTH
    whole = lax.dot_general(
        block, gather, (((0,), (0,)), ((), ())), preferred_element_type=jnp.float32
    )
    last = jnp.zeros((TAIL, LOCAL_BINS * LANES), jnp.float32)
    for s in range(SEG_LOCAL):
        moved = whole[TAIL * s : TAIL * (s + 1)]
        moved = pltpu.roll(moved, (16 * s - USED) % (LOCAL_BINS * LANES), 1)
        last = jnp.where((lane >= 16 * s) & (lane < 16 * s + 16), moved, last)
    return jnp.concatenate([whole, last], 0).astype(jnp.bfloat16)


def turn_kernel(near_ref, mine_ref, far_ref, gather_ref, out_ref):
    for n, ref in enumerate((near_ref, mine_ref, far_ref)):
        for i in range(2):
            block = ref[:, i].reshape(TM * ROWS, LANES)
            for order in range(2):
                out_ref[2 * n + i, order] = turned(block, gather_ref[order])


def turn(near, mine, far, gather):
    shape = (SLOTS - 1, 2, WIDTH, LOCAL_BINS * LANES)
    return pl.pallas_call(
        turn_kernel,
        in_specs=[pl.BlockSpec(memory_space=pltpu.VMEM)] * 4,
        out_specs=pl.BlockSpec(memory_space=pltpu.VMEM),
        out_shape=jax.ShapeDtypeStruct(shape, jnp.bfloat16),
        compiler_params=pltpu.CompilerParams(vmem_limit_bytes=SCOPE),
        cost_estimate=pl.CostEstimate(flops=300_000_000, bytes_accessed=3_000_000, transcendentals=0),
    )(near, mine, far, gather)


def stack_kernel(
    offset_ref, valid_ref, odd_ref, ready_ref, edge_ref, gather_ref, right_ref, out_hbm,
    last_ref, out_ref, sems,
):
    odd = odd_ref[0]
    block = edge_ref[...].reshape(TM * ROWS, LANES)
    for order in range(2):
        last_ref[order] = turned(block, gather_ref[order])
    places = []
    for p in range(SLOTS):
        d = offset_ref[0, p]
        at_even = jnp.where(d == -3, 6, d + 2)
        at_odd = jnp.where(
            d == 3, 6, jnp.where(d <= -2, d + 7, jnp.where(d <= 0, d + 3, d - 1))
        )
        places.append(jnp.where(odd == 1, at_odd, at_even))
    column = lax.broadcasted_iota(jnp.int32, (1, 2 * SPAN), 1)
    weight = jnp.zeros((1, 2 * SPAN), jnp.float32)
    for p in range(SLOTS):
        here = (column >= WIDTH * p) & (column < WIDTH * (p + 1))
        weight = jnp.where(here, valid_ref[0, p].astype(jnp.float32), weight)
    weight = weight * (1.0 / math.sqrt(SEG_LOCAL * TM))
    zero = jnp.zeros((DEPTH, LANES), jnp.bfloat16)
    copies = []
    for f in range(LOCAL_BINS):
        tile = slice(LANES * f, LANES * (f + 1))

        def picked(p):
            held = ready_ref[jnp.minimum(places[p], SLOTS - 2), p % 2, :, tile]
            return jnp.where(places[p] == SLOTS - 1, last_ref[p % 2, :, tile], held)

        tiles = [
            picked(p) + picked(p + 1) if p + 1 < SLOTS else picked(p) for p in range(0, SLOTS, 2)
        ]
        left = jnp.concatenate(
            [jnp.concatenate(tiles[:2], 1), jnp.concatenate(tiles[2:], 1)], 0
        )
        for part in range(2):
            rows = []
            for j in range(4):
                here = [right_ref[f, part, j, :, :LANES], right_ref[f, part, j, :, LANES:]]
                rows.append(jnp.concatenate([zero] * j + here + [zero] * (3 - j), 1))
            product = jnp.dot(
                left, jnp.concatenate(rows, 0), preferred_element_type=jnp.float32
            )
            out_ref[part, f, :, :SPAN] = (product[:WIDTH] * weight[:, :SPAN]).astype(jnp.bfloat16)
            out_ref[part, f, :, SPAN:] = (
                product[WIDTH:, : SLOTS * WIDTH - SPAN] * weight[:, SPAN : SLOTS * WIDTH]
            ).astype(jnp.bfloat16)
            copy = pltpu.make_async_copy(
                out_ref.at[part, f], out_hbm.at[part, f], sems.at[part, f]
            )
            copy.start()
            copies.append(copy)
    for copy in copies:
        copy.wait()


def stack(offsets, valid, odd, ready, edge, gather, right):
    whole = pl.BlockSpec(memory_space=pltpu.VMEM)
    scalars = pl.BlockSpec(memory_space=pltpu.SMEM)
    shape = (2, LOCAL_BINS, WIDTH, SLOTS * WIDTH)
    return pl.pallas_call(
        stack_kernel,
        in_specs=[scalars] * 3 + [whole] * 4,
        out_specs=pl.BlockSpec(memory_space=pltpu.HBM),
        out_shape=jax.ShapeDtypeStruct(shape, jnp.bfloat16),
        scratch_shapes=[
            pltpu.VMEM((2, WIDTH, LOCAL_BINS * LANES), jnp.bfloat16),
            pltpu.VMEM(shape, jnp.bfloat16),
            pltpu.SemaphoreType.DMA((2, LOCAL_BINS)),
        ],
        compiler_params=pltpu.CompilerParams(vmem_limit_bytes=SCOPE),
    )(offsets, valid, odd, ready, edge, gather, right)


def per_device(records, partner, valid):
    blocks = lax.axis_size("pair") * 2
    chan = ("pair", "side")
    side = lax.axis_index("side")
    table = jnp.asarray(spectra_table(records.shape[2]))
    gather, own = (jnp.asarray(x) for x in gather_tables())

    def fetch(array, even, odd):
        route = [((c + (odd if c % 2 else even)) % blocks, c) for c in range(blocks)]
        return lax.ppermute(array, chan, route)

    white = whiten(records, table)
    mine = lax.all_to_all(
        white.reshape(2 * TM, ROWS, LANES), ("tm", "side"), 0, 0, tiled=True
    ).reshape(TM, 2, ROWS, LANES)
    near = fetch(mine, -1, 1)
    far = fetch(mine, 2, -2)
    edge = fetch(lax.dynamic_index_in_dim(far, side, 1, keepdims=False), -1, 1)
    offsets = partner - (lax.axis_index("pair") * 2 + side)
    odd = side.reshape(1)
    right = spread(odd, mine, own)
    ready = turn(near, mine, far, gather)
    result = stack(offsets, valid, odd, ready, edge, gather, right)
    return jnp.transpose(result, (0, 1, 3, 2))


def solution(mesh):
    tm, chan = mesh.shape["tm"], mesh.shape["chan"]
    paired = Mesh(mesh.devices.reshape(tm, chan // 2, 2), ("tm", "pair", "side"))
    blocks = ("pair", "side")
    return jax.shard_map(
        per_device,
        mesh=paired,
        in_specs=(P("tm", blocks, None), P(blocks, None), P(blocks, None)),
        out_specs=P(None, "tm", blocks, None),
        check_vma=False,
    )
```

```python
import functools
import math

import jax
import jax.numpy as jnp
import numpy as np
from jax import lax
from jax.experimental import pallas as pl
from jax.experimental.pallas import tpu as pltpu
from jax.sharding import Mesh
from jax.sharding import PartitionSpec as P

BINS = 32
REACH = 3
SLOTS = 7
WIDTH = 160
LANES = 128
TAIL = WIDTH - LANES
TM = 8
SEG_LOCAL = 3
LOCAL_BINS = BINS // TM
ROWS = 32
DEPTH = 64
USED = 2 * SEG_LOCAL * TM
SPAN = 4 * WIDTH
CHUNK = 512
SCOPE = 32 << 20
SPARE = 7
WHOLE = 54_800_000


def spectra_table(length):
    times = np.arange(length, dtype=np.int64)
    freqs = 60 + 10 * np.arange(BINS, dtype=np.int64)
    phase = (freqs[:, None] * times[None, :]) % length
    angle = phase.astype(np.float32) * np.float32(2.0 * math.pi / length)
    both = np.stack([np.cos(angle), -np.sin(angle)], 0)
    both = both.reshape(2, TM, LOCAL_BINS, length).transpose(1, 0, 2, 3)
    table = both.reshape(1, 2 * BINS, length).astype(jnp.bfloat16)
    return np.concatenate([table, np.zeros((SPARE, 2 * BINS, length), table.dtype)], 0)


def source_row(seg, part, bin_, owner):
    return owner * ROWS + (8 * SEG_LOCAL if seg is None else 8 * seg) + part * LOCAL_BINS + bin_


def depth_rows():
    rows = [(s, t, r) for s in range(SEG_LOCAL) for t in range(TM) for r in range(2)]
    return rows + [(None, t, r) for t in range(TM) for r in range(2)]


def gather_tables():
    rows = depth_rows()
    other = np.zeros((2, TM * ROWS, LOCAL_BINS * LANES), np.float32)
    own = np.zeros((LOCAL_BINS, 2, DEPTH, TM * ROWS), np.float32)
    for f in range(LOCAL_BINS):
        for k, (s, t, r) in enumerate(rows):
            for order in range(2):
                other[order, source_row(s, r, f, t), f * LANES + order * DEPTH + k] = 1
            own[f, 0, k, source_row(s, r, f, t)] = 1
            own[f, 1, k, source_row(s, 1 - r, f, t)] = 1 if r == 0 else -1
    return other.astype(jnp.bfloat16), own.reshape(LOCAL_BINS, 2 * DEPTH, -1).astype(jnp.bfloat16)


def whiten_kernel(table_hbm, records_hbm, out_ref, table_ref, records_ref, sems):
    length = records_ref.shape[2]
    edges = list(range(0, length, CHUNK)) + [length]
    cuts = [slice(a, b) for a, b in zip(edges[:-1], edges[1:])]
    copies = []
    for i, cut in enumerate(cuts):
        part = pl.ds(cut.start, cut.stop - cut.start)
        if i == 0:
            copies.append(pltpu.make_async_copy(table_hbm.at[0], table_ref, sems.at[len(cuts)]))
        copies.append(
            pltpu.make_async_copy(
                records_hbm.at[:, :, part], records_ref.at[:, :, part], sems.at[i]
            )
        )
    for copy in copies:
        copy.start()
    copies[0].wait()
    total = None
    for i, cut in enumerate(cuts):
        copies[i + 1].wait()
        product = lax.dot_general(
            table_ref[:, cut],
            records_ref[:, :, cut].reshape(SEG_LOCAL * WIDTH, cut.stop - cut.start),
            (((1,), (1,)), ((), ())),
            preferred_element_type=jnp.float32,
        )
        total = product if total is None else total + product
    tails = None
    for s in range(SEG_LOCAL):
        spectrum = total[:, WIDTH * s : WIDTH * (s + 1)]
        power = jnp.mean(spectrum * spectrum, axis=0, keepdims=True)
        white = spectrum * lax.rsqrt(power + 1e-06)
        main = white[:, :LANES].astype(jnp.bfloat16).reshape(TM, 8, LANES)
        last = jnp.pad(white[:, LANES:], ((0, 0), (0, LANES - TAIL)))
        tails = last if s == 0 else tails + pltpu.roll(last, TAIL * s, 1)
        for copy in range(2):
            out_ref[:, copy, 8 * s : 8 * s + 8, :] = main
    tails = tails.astype(jnp.bfloat16).reshape(TM, 8, LANES)
    for copy in range(2):
        out_ref[:, copy, 8 * SEG_LOCAL :, :] = tails


def whiten(records, table):
    cuts = -(-records.shape[2] // CHUNK)
    return pl.pallas_call(
        whiten_kernel,
        in_specs=[pl.BlockSpec(memory_space=pltpu.HBM)] * 2,
        out_specs=pl.BlockSpec(memory_space=pltpu.VMEM),
        out_shape=jax.ShapeDtypeStruct((TM, 2, ROWS, LANES), jnp.bfloat16),
        scratch_shapes=[
            pltpu.VMEM(table.shape[1:], jnp.bfloat16),
            pltpu.VMEM(records.shape, jnp.bfloat16),
            pltpu.SemaphoreType.DMA((cuts + 1,)),
        ],
        compiler_params=pltpu.CompilerParams(vmem_limit_bytes=WHOLE),
    )(table, records)


def spread_kernel(odd_ref, mine_ref, own_ref, out_ref):
    own = jnp.where(odd_ref[0] == 1, mine_ref[:, 1], mine_ref[:, 0]).reshape(TM * ROWS, LANES)
    lane = lax.broadcasted_iota(jnp.int32, (USED, LANES), 1)
    fill = jnp.zeros((DEPTH - USED, LANES), jnp.bfloat16)
    for f in range(LOCAL_BINS):
        ordered = jnp.dot(own_ref[f], own, preferred_element_type=jnp.float32)
        for part in range(2):
            rows = ordered[DEPTH * part : DEPTH * (part + 1)]
            main, last = rows[:USED], rows[USED:]
            turns = [last if m == 0 else pltpu.roll(last, TAIL * m, 1) for m in range(4)]
            for j in range(4):
                moved = main if j == 0 else pltpu.roll(main, TAIL * j, 1)
                ends = jnp.concatenate([turns[(j - s) % 4] for s in range(SEG_LOCAL)], 0)
                low = jnp.where(lane >= TAIL * j, moved, 0.0)
                high = jnp.where(
                    lane < TAIL * j, moved, jnp.where(lane < TAIL * (j + 1), ends, 0.0)
                )
                for half, x in enumerate((low, high)):
                    tile = slice(LANES * half, LANES * (half + 1))
                    out_ref[f, part, j, :USED, tile] = x.astype(jnp.bfloat16)
                    out_ref[f, part, j, USED:, tile] = fill


def spread(odd, mine, own):
    shape = (LOCAL_BINS, 2, 4, DEPTH, 2 * LANES)
    return pl.pallas_call(
        spread_kernel,
        in_specs=[pl.BlockSpec(memory_space=pltpu.SMEM)]
        + [pl.BlockSpec(memory_space=pltpu.VMEM)] * 2,
        out_specs=pl.BlockSpec(memory_space=pltpu.VMEM),
        out_shape=jax.ShapeDtypeStruct(shape, jnp.bfloat16),
        compiler_params=pltpu.CompilerParams(vmem_limit_bytes=SCOPE),
        cost_estimate=pl.CostEstimate(flops=70_000_000, bytes_accessed=3_000_000, transcendentals=0),
    )(odd, mine, own)


def turned(block, gather):
    lane = lax.broadcasted_iota(jnp.int32, (TAIL, LOCAL_BINS * LANES), 1) % DEPTH
    whole = lax.dot_general(
        block, gather, (((0,), (0,)), ((), ())), preferred_element_type=jnp.float32
    )
    last = jnp.zeros((TAIL, LOCAL_BINS * LANES), jnp.float32)
    for s in range(SEG_LOCAL):
        moved = whole[TAIL * s : TAIL * (s + 1)]
        moved = pltpu.roll(moved, (16 * s - USED) % (LOCAL_BINS * LANES), 1)
        last = jnp.where((lane >= 16 * s) & (lane < 16 * s + 16), moved, last)
    return jnp.concatenate([whole, last], 0).astype(jnp.bfloat16)


def turn_kernel(near_ref, mine_ref, gather_ref, out_ref):
    for n, ref in enumerate((near_ref, mine_ref)):
        for i in range(2):
            block = ref[:, i].reshape(TM * ROWS, LANES)
            for order in range(2):
                out_ref[2 * n + i, order] = turned(block, gather_ref[order])


def turn(near, mine, gather):
    shape = (4, 2, WIDTH, LOCAL_BINS * LANES)
    return pl.pallas_call(
        turn_kernel,
        in_specs=[pl.BlockSpec(memory_space=pltpu.VMEM)] * 3,
        out_specs=pl.BlockSpec(memory_space=pltpu.VMEM),
        out_shape=jax.ShapeDtypeStruct(shape, jnp.bfloat16),
        compiler_params=pltpu.CompilerParams(vmem_limit_bytes=SCOPE),
        cost_estimate=pl.CostEstimate(flops=200_000_000, bytes_accessed=3_000_000, transcendentals=0),
    )(near, mine, gather)


def stack_kernel(
    offset_ref, valid_ref, odd_ref, ready_ref, far_ref, edge_ref, gather_ref, right_ref, out_hbm,
    last_ref, out_ref, sems,
):
    odd = odd_ref[0]
    for n, block in enumerate((far_ref[:, 0], far_ref[:, 1], edge_ref[...])):
        for order in range(2):
            last_ref[n, order] = turned(block.reshape(TM * ROWS, LANES), gather_ref[order])
    places = []
    for p in range(SLOTS):
        d = offset_ref[0, p]
        at_even = jnp.where(d == -3, 6, d + 2)
        at_odd = jnp.where(
            d == 3, 6, jnp.where(d <= -2, d + 7, jnp.where(d <= 0, d + 3, d - 1))
        )
        places.append(jnp.where(odd == 1, at_odd, at_even))
    column = lax.broadcasted_iota(jnp.int32, (1, 2 * SPAN), 1)
    weight = jnp.zeros((1, 2 * SPAN), jnp.float32)
    for p in range(SLOTS):
        here = (column >= WIDTH * p) & (column < WIDTH * (p + 1))
        weight = jnp.where(here, valid_ref[0, p].astype(jnp.float32), weight)
    weight = weight * (1.0 / math.sqrt(SEG_LOCAL * TM))
    zero = jnp.zeros((DEPTH, LANES), jnp.bfloat16)
    copies = []
    for f in range(LOCAL_BINS):
        tile = slice(LANES * f, LANES * (f + 1))

        def picked(p):
            held = ready_ref[jnp.minimum(places[p], 3), p % 2, :, tile]
            late = last_ref[jnp.maximum(places[p] - 4, 0), p % 2, :, tile]
            return jnp.where(places[p] >= 4, late, held)

        tiles = [
            picked(p) + picked(p + 1) if p + 1 < SLOTS else picked(p) for p in range(0, SLOTS, 2)
        ]
        left = jnp.concatenate(
            [jnp.concatenate(tiles[:2], 1), jnp.concatenate(tiles[2:], 1)], 0
        )
        for part in range(2):
            rows = []
            for j in range(4):
                here = [right_ref[f, part, j, :, :LANES], right_ref[f, part, j, :, LANES:]]
                rows.append(jnp.concatenate([zero] * j + here + [zero] * (3 - j), 1))
            product = jnp.dot(
                left, jnp.concatenate(rows, 0), preferred_element_type=jnp.float32
            )
            out_ref[part, f, :, :SPAN] = (product[:WIDTH] * weight[:, :SPAN]).astype(jnp.bfloat16)
            out_ref[part, f, :, SPAN:] = (
                product[WIDTH:, : SLOTS * WIDTH - SPAN] * weight[:, SPAN : SLOTS * WIDTH]
            ).astype(jnp.bfloat16)
            copy = pltpu.make_async_copy(
                out_ref.at[part, f], out_hbm.at[part, f], sems.at[part, f]
            )
            copy.start()
            copies.append(copy)
    for copy in copies:
        copy.wait()


def stack(offsets, valid, odd, ready, far, edge, gather, right):
    whole = pl.BlockSpec(memory_space=pltpu.VMEM)
    scalars = pl.BlockSpec(memory_space=pltpu.SMEM)
    shape = (2, LOCAL_BINS, WIDTH, SLOTS * WIDTH)
    return pl.pallas_call(
        stack_kernel,
        in_specs=[scalars] * 3 + [whole] * 5,
        out_specs=pl.BlockSpec(memory_space=pltpu.HBM),
        out_shape=jax.ShapeDtypeStruct(shape, jnp.bfloat16),
        scratch_shapes=[
            pltpu.VMEM((3, 2, WIDTH, LOCAL_BINS * LANES), jnp.bfloat16),
            pltpu.VMEM(shape, jnp.bfloat16),
            pltpu.SemaphoreType.DMA((2, LOCAL_BINS)),
        ],
        compiler_params=pltpu.CompilerParams(vmem_limit_bytes=SCOPE),
    )(offsets, valid, odd, ready, far, edge, gather, right)


def per_device(records, partner, valid):
    blocks = lax.axis_size("pair") * 2
    chan = ("pair", "side")
    side = lax.axis_index("side")
    table = jnp.asarray(spectra_table(records.shape[2]))
    gather, own = (jnp.asarray(x) for x in gather_tables())

    def fetch(array, even, odd):
        source = {c: c + (odd if c % 2 else even) for c in range(blocks)}
        last = blocks - 1
        if even == 2:
            source[1], source[last - 1] = 0, last
        elif even == 1:
            pass
        elif even == -3:
            source[0], source[2], source[last], source[last - 2] = 2, 0, last - 2, last
        else:
            source[0], source[2] = 1, 0
            source[last], source[last - 2] = last - 1, last
        return lax.ppermute(array, chan, [(f, c) for c, f in source.items()])

    white = whiten(records, table)
    mine = lax.all_to_all(
        white.reshape(2 * TM, ROWS, LANES), ("tm", "side"), 0, 0, tiled=True
    ).reshape(TM, 2, ROWS, LANES)
    near = fetch(mine, -1, 1)
    edge = fetch(lax.dynamic_index_in_dim(mine, side, 1, keepdims=False), -3, 3)
    far = fetch(near, 1, -1)
    offsets = partner - (lax.axis_index("pair") * 2 + side)
    odd = side.reshape(1)
    right = spread(odd, mine, own)
    ready = turn(near, mine, gather)
    result = stack(offsets, valid, odd, ready, far, edge, gather, right)
    return jnp.transpose(result, (0, 1, 3, 2))


def solution(mesh):
    tm, chan = mesh.shape["tm"], mesh.shape["chan"]
    paired = Mesh(mesh.devices.reshape(tm, chan // 2, 2), ("tm", "pair", "side"))
    blocks = ("pair", "side")
    return jax.shard_map(
        per_device,
        mesh=paired,
        in_specs=(P("tm", blocks, None), P(blocks, None), P(blocks, None)),
        out_specs=P(None, "tm", blocks, None),
        check_vma=False,
    )
```

```python
import functools
import math

import jax
import jax.numpy as jnp
import numpy as np
from jax import lax
from jax.experimental import pallas as pl
from jax.experimental.pallas import tpu as pltpu
from jax.sharding import Mesh
from jax.sharding import PartitionSpec as P

BINS = 32
REACH = 3
SLOTS = 7
WIDTH = 160
LANES = 128
TAIL = WIDTH - LANES
TM = 8
SEG_LOCAL = 3
LOCAL_BINS = BINS // TM
ROWS = 32
DEPTH = 64
USED = 2 * SEG_LOCAL * TM
SPAN = 4 * WIDTH
CHUNK = 512
SCOPE = 32 << 20
SPARE = 7
WHOLE = 54_800_000


def spectra_table(length):
    times = np.arange(length, dtype=np.int64)
    freqs = 60 + 10 * np.arange(BINS, dtype=np.int64)
    phase = (freqs[:, None] * times[None, :]) % length
    angle = phase.astype(np.float32) * np.float32(2.0 * math.pi / length)
    both = np.stack([np.cos(angle), -np.sin(angle)], 0)
    both = both.reshape(2, TM, LOCAL_BINS, length).transpose(1, 0, 2, 3)
    table = both.reshape(1, 2 * BINS, length).astype(jnp.bfloat16)
    return np.concatenate([table, np.zeros((SPARE, 2 * BINS, length), table.dtype)], 0)


def source_row(seg, part, bin_, owner):
    return owner * ROWS + (8 * SEG_LOCAL if seg is None else 8 * seg) + part * LOCAL_BINS + bin_


def depth_rows():
    rows = [(s, t, r) for s in range(SEG_LOCAL) for t in range(TM) for r in range(2)]
    return rows + [(None, t, r) for t in range(TM) for r in range(2)]


def gather_tables():
    rows = depth_rows()
    other = np.zeros((2, TM * ROWS, LOCAL_BINS * LANES), np.float32)
    own = np.zeros((LOCAL_BINS, 2, DEPTH, TM * ROWS), np.float32)
    for f in range(LOCAL_BINS):
        for k, (s, t, r) in enumerate(rows):
            for order in range(2):
                other[order, source_row(s, r, f, t), f * LANES + order * DEPTH + k] = 1
            own[f, 0, k, source_row(s, r, f, t)] = 1
            own[f, 1, k, source_row(s, 1 - r, f, t)] = 1 if r == 0 else -1
    return other.astype(jnp.bfloat16), own.reshape(LOCAL_BINS, 2 * DEPTH, -1).astype(jnp.bfloat16)


def whiten_kernel(table_hbm, records_hbm, out_ref, table_ref, records_ref, sems):
    length = records_ref.shape[2]
    edges = list(range(0, length, CHUNK)) + [length]
    cuts = [slice(a, b) for a, b in zip(edges[:-1], edges[1:])]
    copies = []
    for i, cut in enumerate(cuts):
        part = pl.ds(cut.start, cut.stop - cut.start)
        if i == 0:
            copies.append(pltpu.make_async_copy(table_hbm.at[0], table_ref, sems.at[len(cuts)]))
        copies.append(
            pltpu.make_async_copy(
                records_hbm.at[:, :, part], records_ref.at[:, :, part], sems.at[i]
            )
        )
    for copy in copies:
        copy.start()
    copies[0].wait()
    total = None
    for i, cut in enumerate(cuts):
        copies[i + 1].wait()
        product = lax.dot_general(
            table_ref[:, cut],
            records_ref[:, :, cut].reshape(SEG_LOCAL * WIDTH, cut.stop - cut.start),
            (((1,), (1,)), ((), ())),
            preferred_element_type=jnp.float32,
        )
        total = product if total is None else total + product
    tails = None
    for s in range(SEG_LOCAL):
        spectrum = total[:, WIDTH * s : WIDTH * (s + 1)]
        power = jnp.mean(spectrum * spectrum, axis=0, keepdims=True)
        white = spectrum * lax.rsqrt(power + 1e-06)
        main = white[:, :LANES].astype(jnp.bfloat16).reshape(TM, 8, LANES)
        last = jnp.pad(white[:, LANES:], ((0, 0), (0, LANES - TAIL)))
        tails = last if s == 0 else tails + pltpu.roll(last, TAIL * s, 1)
        for copy in range(2):
            out_ref[:, copy, 8 * s : 8 * s + 8, :] = main
    tails = tails.astype(jnp.bfloat16).reshape(TM, 8, LANES)
    for copy in range(2):
        out_ref[:, copy, 8 * SEG_LOCAL :, :] = tails


def whiten(records, table):
    cuts = -(-records.shape[2] // CHUNK)
    return pl.pallas_call(
        whiten_kernel,
        in_specs=[pl.BlockSpec(memory_space=pltpu.HBM)] * 2,
        out_specs=pl.BlockSpec(memory_space=pltpu.VMEM),
        out_shape=jax.ShapeDtypeStruct((TM, 2, ROWS, LANES), jnp.bfloat16),
        scratch_shapes=[
            pltpu.VMEM(table.shape[1:], jnp.bfloat16),
            pltpu.VMEM(records.shape, jnp.bfloat16),
            pltpu.SemaphoreType.DMA((cuts + 1,)),
        ],
        compiler_params=pltpu.CompilerParams(vmem_limit_bytes=WHOLE),
    )(table, records)


def spread_kernel(odd_ref, mine_ref, own_ref, out_ref, alone_ref):
    alone = jnp.where(odd_ref[0] == 1, mine_ref[:, 1], mine_ref[:, 0])
    alone_ref[...] = alone
    own = alone.reshape(TM * ROWS, LANES)
    lane = lax.broadcasted_iota(jnp.int32, (USED, LANES), 1)
    fill = jnp.zeros((DEPTH - USED, LANES), jnp.bfloat16)
    for f in range(LOCAL_BINS):
        ordered = jnp.dot(own_ref[f], own, preferred_element_type=jnp.float32)
        for part in range(2):
            rows = ordered[DEPTH * part : DEPTH * (part + 1)]
            main, last = rows[:USED], rows[USED:]
            turns = [last if m == 0 else pltpu.roll(last, TAIL * m, 1) for m in range(4)]
            for j in range(4):
                moved = main if j == 0 else pltpu.roll(main, TAIL * j, 1)
                ends = jnp.concatenate([turns[(j - s) % 4] for s in range(SEG_LOCAL)], 0)
                low = jnp.where(lane >= TAIL * j, moved, 0.0)
                high = jnp.where(
                    lane < TAIL * j, moved, jnp.where(lane < TAIL * (j + 1), ends, 0.0)
                )
                for half, x in enumerate((low, high)):
                    tile = slice(LANES * half, LANES * (half + 1))
                    out_ref[f, part, j, :USED, tile] = x.astype(jnp.bfloat16)
                    out_ref[f, part, j, USED:, tile] = fill


def spread(odd, mine, own):
    shape = (LOCAL_BINS, 2, 4, DEPTH, 2 * LANES)
    return pl.pallas_call(
        spread_kernel,
        in_specs=[pl.BlockSpec(memory_space=pltpu.SMEM)]
        + [pl.BlockSpec(memory_space=pltpu.VMEM)] * 2,
        out_specs=[pl.BlockSpec(memory_space=pltpu.VMEM)] * 2,
        out_shape=[
            jax.ShapeDtypeStruct(shape, jnp.bfloat16),
            jax.ShapeDtypeStruct((TM, ROWS, LANES), jnp.bfloat16),
        ],
        compiler_params=pltpu.CompilerParams(vmem_limit_bytes=SCOPE),
        cost_estimate=pl.CostEstimate(flops=70_000_000, bytes_accessed=3_000_000, transcendentals=0),
    )(odd, mine, own)


def turned(block, gather):
    lane = lax.broadcasted_iota(jnp.int32, (TAIL, LOCAL_BINS * LANES), 1) % DEPTH
    whole = lax.dot_general(
        block, gather, (((0,), (0,)), ((), ())), preferred_element_type=jnp.float32
    )
    last = jnp.zeros((TAIL, LOCAL_BINS * LANES), jnp.float32)
    for s in range(SEG_LOCAL):
        moved = whole[TAIL * s : TAIL * (s + 1)]
        moved = pltpu.roll(moved, (16 * s - USED) % (LOCAL_BINS * LANES), 1)
        last = jnp.where((lane >= 16 * s) & (lane < 16 * s + 16), moved, last)
    return jnp.concatenate([whole, last], 0).astype(jnp.bfloat16)


def turn_kernel(valid_ref, near_ref, mine_ref, gather_ref, out_ref, weight_ref):
    column = lax.broadcasted_iota(jnp.int32, (1, 2 * SPAN), 1)
    weight = jnp.zeros((1, 2 * SPAN), jnp.float32)
    for p in range(SLOTS):
        here = (column >= WIDTH * p) & (column < WIDTH * (p + 1))
        weight = jnp.where(here, valid_ref[0, p].astype(jnp.float32), weight)
    weight = weight * (1.0 / math.sqrt(SEG_LOCAL * TM))
    weight_ref[...] = weight
    for n, ref in enumerate((near_ref, mine_ref)):
        for i in range(2):
            block = ref[:, i].reshape(TM * ROWS, LANES)
            for order in range(2):
                out_ref[2 * n + i, order] = turned(block, gather_ref[order])


def turn(valid, near, mine, gather):
    shape = (4, 2, WIDTH, LOCAL_BINS * LANES)
    return pl.pallas_call(
        turn_kernel,
        in_specs=[pl.BlockSpec(memory_space=pltpu.VMEM)] * 4,
        out_specs=[pl.BlockSpec(memory_space=pltpu.VMEM)] * 2,
        out_shape=[
            jax.ShapeDtypeStruct(shape, jnp.bfloat16),
            jax.ShapeDtypeStruct((1, 2 * SPAN), jnp.float32),
        ],
        compiler_params=pltpu.CompilerParams(vmem_limit_bytes=SCOPE),
        cost_estimate=pl.CostEstimate(flops=200_000_000, bytes_accessed=3_000_000, transcendentals=0),
    )(valid, near, mine, gather)


def stack_kernel(
    places_ref, weight_ref, ready_ref, far_ref, edge_ref, gather_ref, right_ref, out_hbm,
    last_ref, out_ref, sems,
):
    places = [places_ref[0, p] for p in range(SLOTS)]
    for n, block in enumerate((far_ref[:, 0], far_ref[:, 1], edge_ref[...])):
        for order in range(2):
            last_ref[n, order] = turned(block.reshape(TM * ROWS, LANES), gather_ref[order])
    weight = weight_ref[...]
    zero = jnp.zeros((DEPTH, LANES), jnp.bfloat16)
    copies = []
    for f in range(LOCAL_BINS):
        tile = slice(LANES * f, LANES * (f + 1))

        def picked(p):
            held = ready_ref[jnp.minimum(places[p], 3), p % 2, :, tile]
            late = last_ref[jnp.maximum(places[p] - 4, 0), p % 2, :, tile]
            return jnp.where(places[p] >= 4, late, held)

        tiles = [
            picked(p) + picked(p + 1) if p + 1 < SLOTS else picked(p) for p in range(0, SLOTS, 2)
        ]
        left = jnp.concatenate(
            [jnp.concatenate(tiles[:2], 1), jnp.concatenate(tiles[2:], 1)], 0
        )
        for part in range(2):
            rows = []
            for j in range(4):
                here = [right_ref[f, part, j, :, :LANES], right_ref[f, part, j, :, LANES:]]
                rows.append(jnp.concatenate([zero] * j + here + [zero] * (3 - j), 1))
            product = jnp.dot(
                left, jnp.concatenate(rows, 0), preferred_element_type=jnp.float32
            )
            out_ref[part, f, :, :SPAN] = (product[:WIDTH] * weight[:, :SPAN]).astype(jnp.bfloat16)
            out_ref[part, f, :, SPAN:] = (
                product[WIDTH:, : SLOTS * WIDTH - SPAN] * weight[:, SPAN : SLOTS * WIDTH]
            ).astype(jnp.bfloat16)
            copy = pltpu.make_async_copy(
                out_ref.at[part, f], out_hbm.at[part, f], sems.at[part, f]
            )
            copy.start()
            copies.append(copy)
    for copy in copies:
        copy.wait()


def stack(places, weight, ready, far, edge, gather, right):
    whole = pl.BlockSpec(memory_space=pltpu.VMEM)
    shape = (2, LOCAL_BINS, WIDTH, SLOTS * WIDTH)
    return pl.pallas_call(
        stack_kernel,
        in_specs=[whole] * 7,
        out_specs=pl.BlockSpec(memory_space=pltpu.HBM),
        out_shape=jax.ShapeDtypeStruct(shape, jnp.bfloat16),
        scratch_shapes=[
            pltpu.VMEM((3, 2, WIDTH, LOCAL_BINS * LANES), jnp.bfloat16),
            pltpu.VMEM(shape, jnp.bfloat16),
            pltpu.SemaphoreType.DMA((2, LOCAL_BINS)),
        ],
        compiler_params=pltpu.CompilerParams(vmem_limit_bytes=SCOPE),
    )(places, weight, ready, far, edge, gather, right)


def place_of(partner, me, side):
    d = partner - me
    at_even = jnp.where(d == -3, 6, d + 2)
    at_odd = jnp.where(d == 3, 6, jnp.where(d <= -2, d + 7, jnp.where(d <= 0, d + 3, d - 1)))
    return jnp.where(side == 1, at_odd, at_even)


def per_device(records, partner, valid):
    blocks = lax.axis_size("pair") * 2
    chan = ("pair", "side")
    side = lax.axis_index("side")
    table = jnp.asarray(spectra_table(records.shape[2]))
    gather, own = (jnp.asarray(x) for x in gather_tables())

    def fetch(array, even, odd):
        source = {c: c + (odd if c % 2 else even) for c in range(blocks)}
        last = blocks - 1
        if even == 2:
            source[1], source[last - 1] = 0, last
        elif even == 1:
            pass
        elif even == -3:
            source[0], source[2], source[last], source[last - 2] = 2, 0, last - 2, last
        else:
            source[0], source[2] = 1, 0
            source[last], source[last - 2] = last - 1, last
        return lax.ppermute(array, chan, [(f, c) for c, f in source.items()])

    white = whiten(records, table)
    mine = lax.all_to_all(
        white.reshape(2 * TM, ROWS, LANES), ("tm", "side"), 0, 0, tiled=True
    ).reshape(TM, 2, ROWS, LANES)
    near = fetch(mine, -1, 1)
    odd = side.reshape(1)
    right, alone = spread(odd, mine, own)
    edge = fetch(alone, -3, 3)
    far = fetch(near, 1, -1)
    me = lax.axis_index("pair") * 2 + side
    ready, weight = turn(valid, near, mine, gather)
    result = stack(place_of(partner, me, side), weight, ready, far, edge, gather, right)
    return jnp.transpose(result, (0, 1, 3, 2))


def solution(mesh):
    tm, chan = mesh.shape["tm"], mesh.shape["chan"]
    paired = Mesh(mesh.devices.reshape(tm, chan // 2, 2), ("tm", "pair", "side"))
    blocks = ("pair", "side")
    return jax.shard_map(
        per_device,
        mesh=paired,
        in_specs=(P("tm", blocks, None), P(blocks, None), P(blocks, None)),
        out_specs=P(None, "tm", blocks, None),
        check_vma=False,
    )
```

```python
import functools
import math

import jax
import jax.numpy as jnp
import numpy as np
from jax import lax
from jax.experimental import pallas as pl
from jax.experimental.pallas import tpu as pltpu
from jax.sharding import Mesh
from jax.sharding import PartitionSpec as P

BINS = 32
REACH = 3
SLOTS = 7
WIDTH = 160
LANES = 128
TAIL = WIDTH - LANES
TM = 8
SEG_LOCAL = 3
LOCAL_BINS = BINS // TM
ROWS = 32
DEPTH = 64
USED = 2 * SEG_LOCAL * TM
SPAN = 4 * WIDTH
CHUNK = 512
SCOPE = 32 << 20
SPARE = 7
WHOLE = 54_800_000


def spectra_table(length):
    times = np.arange(length, dtype=np.int64)
    freqs = 60 + 10 * np.arange(BINS, dtype=np.int64)
    phase = (freqs[:, None] * times[None, :]) % length
    angle = phase.astype(np.float32) * np.float32(2.0 * math.pi / length)
    both = np.stack([np.cos(angle), -np.sin(angle)], 0)
    both = both.reshape(2, TM, LOCAL_BINS, length).transpose(1, 0, 2, 3)
    table = both.reshape(1, 2 * BINS, length).astype(jnp.bfloat16)
    return np.concatenate([table, np.zeros((SPARE, 2 * BINS, length), table.dtype)], 0)


def source_row(seg, part, bin_, owner):
    return owner * ROWS + (8 * SEG_LOCAL if seg is None else 8 * seg) + part * LOCAL_BINS + bin_


def depth_rows():
    rows = [(s, t, r) for s in range(SEG_LOCAL) for t in range(TM) for r in range(2)]
    return rows + [(None, t, r) for t in range(TM) for r in range(2)]


def gather_tables():
    rows = depth_rows()
    other = np.zeros((2, TM * ROWS, LOCAL_BINS * LANES), np.float32)
    own = np.zeros((LOCAL_BINS, 2, DEPTH, TM * ROWS), np.float32)
    for f in range(LOCAL_BINS):
        for k, (s, t, r) in enumerate(rows):
            for order in range(2):
                other[order, source_row(s, r, f, t), f * LANES + order * DEPTH + k] = 1
            own[f, 0, k, source_row(s, r, f, t)] = 1
            own[f, 1, k, source_row(s, 1 - r, f, t)] = 1 if r == 0 else -1
    return other.astype(jnp.bfloat16), own.reshape(LOCAL_BINS, 2 * DEPTH, -1).astype(jnp.bfloat16)


def whiten_kernel(table_hbm, records_hbm, out_ref, table_ref, records_ref, sems):
    length = records_ref.shape[2]
    edges = list(range(0, length, CHUNK)) + [length]
    cuts = [slice(a, b) for a, b in zip(edges[:-1], edges[1:])]
    copies = []
    for i, cut in enumerate(cuts):
        part = pl.ds(cut.start, cut.stop - cut.start)
        copies.append(
            (
                pltpu.make_async_copy(
                    table_hbm.at[0, :, part], table_ref.at[:, part], sems.at[i, 0]
                ),
                pltpu.make_async_copy(
                    records_hbm.at[:, :, part], records_ref.at[:, :, part], sems.at[i, 1]
                ),
            )
        )
    for pair in copies:
        for copy in pair:
            copy.start()
    total = None
    for i, cut in enumerate(cuts):
        for copy in copies[i]:
            copy.wait()
        product = lax.dot_general(
            table_ref[:, cut],
            records_ref[:, :, cut].reshape(SEG_LOCAL * WIDTH, cut.stop - cut.start),
            (((1,), (1,)), ((), ())),
            preferred_element_type=jnp.float32,
        )
        total = product if total is None else total + product
    tails = None
    for s in range(SEG_LOCAL):
        spectrum = total[:, WIDTH * s : WIDTH * (s + 1)]
        power = jnp.mean(spectrum * spectrum, axis=0, keepdims=True)
        white = spectrum * lax.rsqrt(power + 1e-06)
        main = white[:, :LANES].astype(jnp.bfloat16).reshape(TM, 8, LANES)
        last = jnp.pad(white[:, LANES:], ((0, 0), (0, LANES - TAIL)))
        tails = last if s == 0 else tails + pltpu.roll(last, TAIL * s, 1)
        for copy in range(2):
            out_ref[:, copy, 8 * s : 8 * s + 8, :] = main
    tails = tails.astype(jnp.bfloat16).reshape(TM, 8, LANES)
    for copy in range(2):
        out_ref[:, copy, 8 * SEG_LOCAL :, :] = tails


def whiten(records, table):
    cuts = -(-records.shape[2] // CHUNK)
    return pl.pallas_call(
        whiten_kernel,
        in_specs=[pl.BlockSpec(memory_space=pltpu.HBM)] * 2,
        out_specs=pl.BlockSpec(memory_space=pltpu.VMEM),
        out_shape=jax.ShapeDtypeStruct((TM, 2, ROWS, LANES), jnp.bfloat16),
        scratch_shapes=[
            pltpu.VMEM(table.shape[1:], jnp.bfloat16),
            pltpu.VMEM(records.shape, jnp.bfloat16),
            pltpu.SemaphoreType.DMA((cuts, 2)),
        ],
        compiler_params=pltpu.CompilerParams(vmem_limit_bytes=WHOLE),
    )(table, records)


def spread_kernel(odd_ref, mine_ref, own_ref, out_ref, alone_ref):
    alone = jnp.where(odd_ref[0] == 1, mine_ref[:, 1], mine_ref[:, 0])
    alone_ref[...] = alone
    own = alone.reshape(TM * ROWS, LANES)
    lane = lax.broadcasted_iota(jnp.int32, (USED, LANES), 1)
    fill = jnp.zeros((DEPTH - USED, LANES), jnp.bfloat16)
    for f in range(LOCAL_BINS):
        ordered = jnp.dot(own_ref[f], own, preferred_element_type=jnp.float32)
        for part in range(2):
            rows = ordered[DEPTH * part : DEPTH * (part + 1)]
            main, last = rows[:USED], rows[USED:]
            turns = [last if m == 0 else pltpu.roll(last, TAIL * m, 1) for m in range(4)]
            for j in range(4):
                moved = main if j == 0 else pltpu.roll(main, TAIL * j, 1)
                ends = jnp.concatenate([turns[(j - s) % 4] for s in range(SEG_LOCAL)], 0)
                low = jnp.where(lane >= TAIL * j, moved, 0.0)
                high = jnp.where(
                    lane < TAIL * j, moved, jnp.where(lane < TAIL * (j + 1), ends, 0.0)
                )
                for half, x in enumerate((low, high)):
                    tile = slice(LANES * half, LANES * (half + 1))
                    out_ref[f, part, j, :USED, tile] = x.astype(jnp.bfloat16)
                    out_ref[f, part, j, USED:, tile] = fill


def spread(odd, mine, own):
    shape = (LOCAL_BINS, 2, 4, DEPTH, 2 * LANES)
    return pl.pallas_call(
        spread_kernel,
        in_specs=[pl.BlockSpec(memory_space=pltpu.SMEM)]
        + [pl.BlockSpec(memory_space=pltpu.VMEM)] * 2,
        out_specs=[pl.BlockSpec(memory_space=pltpu.VMEM)] * 2,
        out_shape=[
            jax.ShapeDtypeStruct(shape, jnp.bfloat16),
            jax.ShapeDtypeStruct((TM, ROWS, LANES), jnp.bfloat16),
        ],
        compiler_params=pltpu.CompilerParams(vmem_limit_bytes=SCOPE),
        cost_estimate=pl.CostEstimate(flops=70_000_000, bytes_accessed=3_000_000, transcendentals=0),
    )(odd, mine, own)


def turned(block, gather):
    lane = lax.broadcasted_iota(jnp.int32, (TAIL, LOCAL_BINS * LANES), 1) % DEPTH
    whole = lax.dot_general(
        block, gather, (((0,), (0,)), ((), ())), preferred_element_type=jnp.float32
    )
    last = jnp.zeros((TAIL, LOCAL_BINS * LANES), jnp.float32)
    for s in range(SEG_LOCAL):
        moved = whole[TAIL * s : TAIL * (s + 1)]
        moved = pltpu.roll(moved, (16 * s - USED) % (LOCAL_BINS * LANES), 1)
        last = jnp.where((lane >= 16 * s) & (lane < 16 * s + 16), moved, last)
    return jnp.concatenate([whole, last], 0).astype(jnp.bfloat16)


def turn_kernel(valid_ref, near_ref, mine_ref, gather_ref, out_ref, weight_ref):
    column = lax.broadcasted_iota(jnp.int32, (1, 2 * SPAN), 1)
    weight = jnp.zeros((1, 2 * SPAN), jnp.float32)
    for p in range(SLOTS):
        here = (column >= WIDTH * p) & (column < WIDTH * (p + 1))
        weight = jnp.where(here, valid_ref[0, p].astype(jnp.float32), weight)
    weight = weight * (1.0 / math.sqrt(SEG_LOCAL * TM))
    weight_ref[...] = weight
    for n, ref in enumerate((near_ref, mine_ref)):
        for i in range(2):
            block = ref[:, i].reshape(TM * ROWS, LANES)
            for order in range(2):
                out_ref[2 * n + i, order] = turned(block, gather_ref[order])


def turn(valid, near, mine, gather):
    shape = (4, 2, WIDTH, LOCAL_BINS * LANES)
    return pl.pallas_call(
        turn_kernel,
        in_specs=[pl.BlockSpec(memory_space=pltpu.VMEM)] * 4,
        out_specs=[pl.BlockSpec(memory_space=pltpu.VMEM)] * 2,
        out_shape=[
            jax.ShapeDtypeStruct(shape, jnp.bfloat16),
            jax.ShapeDtypeStruct((1, 2 * SPAN), jnp.float32),
        ],
        compiler_params=pltpu.CompilerParams(vmem_limit_bytes=SCOPE),
        cost_estimate=pl.CostEstimate(flops=200_000_000, bytes_accessed=3_000_000, transcendentals=0),
    )(valid, near, mine, gather)


def stack_kernel(
    places_ref, weight_ref, ready_ref, far_ref, edge_ref, gather_ref, right_ref, out_hbm,
    last_ref, out_ref, sems,
):
    places = [places_ref[0, p] for p in range(SLOTS)]
    for n, block in enumerate((far_ref[:, 0], far_ref[:, 1], edge_ref[...])):
        for order in range(2):
            last_ref[n, order] = turned(block.reshape(TM * ROWS, LANES), gather_ref[order])
    weight = weight_ref[...]
    zero = jnp.zeros((DEPTH, LANES), jnp.bfloat16)
    copies = []
    for f in range(LOCAL_BINS):
        tile = slice(LANES * f, LANES * (f + 1))

        def picked(p):
            held = ready_ref[jnp.minimum(places[p], 3), p % 2, :, tile]
            late = last_ref[jnp.maximum(places[p] - 4, 0), p % 2, :, tile]
            return jnp.where(places[p] >= 4, late, held)

        tiles = [
            picked(p) + picked(p + 1) if p + 1 < SLOTS else picked(p) for p in range(0, SLOTS, 2)
        ]
        left = jnp.concatenate(
            [jnp.concatenate(tiles[:2], 1), jnp.concatenate(tiles[2:], 1)], 0
        )
        for part in range(2):
            rows = []
            for j in range(4):
                here = [right_ref[f, part, j, :, :LANES], right_ref[f, part, j, :, LANES:]]
                rows.append(jnp.concatenate([zero] * j + here + [zero] * (3 - j), 1))
            product = jnp.dot(
                left, jnp.concatenate(rows, 0), preferred_element_type=jnp.float32
            )
            out_ref[part, f, :, :SPAN] = (product[:WIDTH] * weight[:, :SPAN]).astype(jnp.bfloat16)
            out_ref[part, f, :, SPAN:] = (
                product[WIDTH:, : SLOTS * WIDTH - SPAN] * weight[:, SPAN : SLOTS * WIDTH]
            ).astype(jnp.bfloat16)
            copy = pltpu.make_async_copy(
                out_ref.at[part, f], out_hbm.at[part, f], sems.at[part, f]
            )
            copy.start()
            copies.append(copy)
    for copy in copies:
        copy.wait()


def stack(places, weight, ready, far, edge, gather, right):
    whole = pl.BlockSpec(memory_space=pltpu.VMEM)
    shape = (2, LOCAL_BINS, WIDTH, SLOTS * WIDTH)
    return pl.pallas_call(
        stack_kernel,
        in_specs=[whole] * 7,
        out_specs=pl.BlockSpec(memory_space=pltpu.HBM),
        out_shape=jax.ShapeDtypeStruct(shape, jnp.bfloat16),
        scratch_shapes=[
            pltpu.VMEM((3, 2, WIDTH, LOCAL_BINS * LANES), jnp.bfloat16),
            pltpu.VMEM(shape, jnp.bfloat16),
            pltpu.SemaphoreType.DMA((2, LOCAL_BINS)),
        ],
        compiler_params=pltpu.CompilerParams(vmem_limit_bytes=SCOPE),
    )(places, weight, ready, far, edge, gather, right)


def place_of(partner, me, side):
    d = partner - me
    at_even = jnp.where(d == -3, 6, d + 2)
    at_odd = jnp.where(d == 3, 6, jnp.where(d <= -2, d + 7, jnp.where(d <= 0, d + 3, d - 1)))
    return jnp.where(side == 1, at_odd, at_even)


def per_device(records, partner, valid):
    blocks = lax.axis_size("pair") * 2
    chan = ("pair", "side")
    side = lax.axis_index("side")
    table = jnp.asarray(spectra_table(records.shape[2]))
    gather, own = (jnp.asarray(x) for x in gather_tables())

    def fetch(array, even, odd):
        source = {c: c + (odd if c % 2 else even) for c in range(blocks)}
        last = blocks - 1
        if even == 2:
            source[1], source[last - 1] = 0, last
        elif even == 1:
            pass
        elif even == -3:
            source[0], source[2], source[last], source[last - 2] = 2, 0, last - 2, last
        else:
            source[0], source[2] = 1, 0
            source[last], source[last - 2] = last - 1, last
        return lax.ppermute(array, chan, [(f, c) for c, f in source.items()])

    white = whiten(records, table)
    mine = lax.all_to_all(
        white.reshape(2 * TM, ROWS, LANES), ("tm", "side"), 0, 0, tiled=True
    ).reshape(TM, 2, ROWS, LANES)
    near = fetch(mine, -1, 1)
    odd = side.reshape(1)
    right, alone = spread(odd, mine, own)
    edge = fetch(alone, -3, 3)
    far = fetch(near, 1, -1)
    me = lax.axis_index("pair") * 2 + side
    ready, weight = turn(valid, near, mine, gather)
    result = stack(place_of(partner, me, side), weight, ready, far, edge, gather, right)
    return jnp.transpose(result, (0, 1, 3, 2))


def solution(mesh):
    tm, chan = mesh.shape["tm"], mesh.shape["chan"]
    paired = Mesh(mesh.devices.reshape(tm, chan // 2, 2), ("tm", "pair", "side"))
    blocks = ("pair", "side")
    return jax.shard_map(
        per_device,
        mesh=paired,
        in_specs=(P("tm", blocks, None), P(blocks, None), P(blocks, None)),
        out_specs=P(None, "tm", blocks, None),
        check_vma=False,
    )
```

```python
import functools
import math

import jax
import jax.numpy as jnp
import numpy as np
from jax import lax
from jax.experimental import pallas as pl
from jax.experimental.pallas import tpu as pltpu
from jax.sharding import Mesh
from jax.sharding import PartitionSpec as P

BINS = 32
REACH = 3
SLOTS = 7
WIDTH = 160
LANES = 128
TAIL = WIDTH - LANES
TM = 8
SEG_LOCAL = 3
LOCAL_BINS = BINS // TM
ROWS = 32
DEPTH = 64
USED = 2 * SEG_LOCAL * TM
SPAN = 4 * WIDTH
CHUNK = 512
SCOPE = 32 << 20
SPARE = 7
WHOLE = 54_800_000


def spectra_table(length):
    times = np.arange(length, dtype=np.int64)
    freqs = 60 + 10 * np.arange(BINS, dtype=np.int64)
    phase = (freqs[:, None] * times[None, :]) % length
    angle = phase.astype(np.float32) * np.float32(2.0 * math.pi / length)
    both = np.stack([np.cos(angle), -np.sin(angle)], 0)
    both = both.reshape(2, TM, LOCAL_BINS, length).transpose(1, 0, 2, 3)
    table = both.reshape(1, 2 * BINS, length).astype(jnp.bfloat16)
    return np.concatenate([table, np.zeros((SPARE, 2 * BINS, length), table.dtype)], 0)


def source_row(seg, part, bin_, owner):
    return owner * ROWS + (8 * SEG_LOCAL if seg is None else 8 * seg) + part * LOCAL_BINS + bin_


def depth_rows():
    rows = [(s, t, r) for s in range(SEG_LOCAL) for t in range(TM) for r in range(2)]
    return rows + [(None, t, r) for t in range(TM) for r in range(2)]


def gather_tables():
    rows = depth_rows()
    other = np.zeros((2, TM * ROWS, LOCAL_BINS * LANES), np.float32)
    own = np.zeros((LOCAL_BINS, 2, DEPTH, TM * ROWS), np.float32)
    for f in range(LOCAL_BINS):
        for k, (s, t, r) in enumerate(rows):
            for order in range(2):
                other[order, source_row(s, r, f, t), f * LANES + order * DEPTH + k] = 1
            own[f, 0, k, source_row(s, r, f, t)] = 1
            own[f, 1, k, source_row(s, 1 - r, f, t)] = 1 if r == 0 else -1
    return other.astype(jnp.bfloat16), own.reshape(LOCAL_BINS, 2 * DEPTH, -1).astype(jnp.bfloat16)


def whiten_kernel(table_hbm, records_hbm, out_ref, table_ref, records_ref, sems):
    length = records_ref.shape[2]
    edges = list(range(0, length, CHUNK)) + [length]
    cuts = [slice(a, b) for a, b in zip(edges[:-1], edges[1:])]
    copies = []
    for i, cut in enumerate(cuts):
        part = pl.ds(cut.start, cut.stop - cut.start)
        copies.append(
            (
                pltpu.make_async_copy(
                    table_hbm.at[0, :, part], table_ref.at[:, part], sems.at[i, 0]
                ),
                pltpu.make_async_copy(
                    records_hbm.at[:, :, part], records_ref.at[:, :, part], sems.at[i, 1]
                ),
            )
        )
    for pair in copies:
        for copy in pair:
            copy.start()
    total = None
    for i, cut in enumerate(cuts):
        for copy in copies[i]:
            copy.wait()
        product = lax.dot_general(
            table_ref[:, cut],
            records_ref[:, :, cut].reshape(SEG_LOCAL * WIDTH, cut.stop - cut.start),
            (((1,), (1,)), ((), ())),
            preferred_element_type=jnp.float32,
        )
        total = product if total is None else total + product
    tails = None
    for s in range(SEG_LOCAL):
        spectrum = total[:, WIDTH * s : WIDTH * (s + 1)]
        power = jnp.mean(spectrum * spectrum, axis=0, keepdims=True)
        white = spectrum * lax.rsqrt(power + 1e-06)
        main = white[:, :LANES].astype(jnp.bfloat16).reshape(TM, 8, LANES)
        last = jnp.pad(white[:, LANES:], ((0, 0), (0, LANES - TAIL)))
        tails = last if s == 0 else tails + pltpu.roll(last, TAIL * s, 1)
        for copy in range(2):
            out_ref[:, copy, 8 * s : 8 * s + 8, :] = main
    tails = tails.astype(jnp.bfloat16).reshape(TM, 8, LANES)
    for copy in range(2):
        out_ref[:, copy, 8 * SEG_LOCAL :, :] = tails


def whiten(records, table):
    cuts = -(-records.shape[2] // CHUNK)
    return pl.pallas_call(
        whiten_kernel,
        in_specs=[pl.BlockSpec(memory_space=pltpu.HBM)] * 2,
        out_specs=pl.BlockSpec(memory_space=pltpu.VMEM),
        out_shape=jax.ShapeDtypeStruct((TM, 2, ROWS, LANES), jnp.bfloat16),
        scratch_shapes=[
            pltpu.VMEM(table.shape[1:], jnp.bfloat16),
            pltpu.VMEM(records.shape, jnp.bfloat16),
            pltpu.SemaphoreType.DMA((cuts, 2)),
        ],
        compiler_params=pltpu.CompilerParams(vmem_limit_bytes=WHOLE),
    )(table, records)


def spread_kernel(odd_ref, mine_ref, own_ref, out_ref, alone_ref):
    alone = jnp.where(odd_ref[0] == 1, mine_ref[:, 1], mine_ref[:, 0])
    alone_ref[...] = alone
    own = alone.reshape(TM * ROWS, LANES)
    lane = lax.broadcasted_iota(jnp.int32, (USED, LANES), 1)
    fill = jnp.zeros((DEPTH - USED, LANES), jnp.bfloat16)
    for f in range(LOCAL_BINS):
        ordered = jnp.dot(own_ref[f], own, preferred_element_type=jnp.float32)
        for part in range(2):
            rows = ordered[DEPTH * part : DEPTH * (part + 1)]
            main, last = rows[:USED], rows[USED:]
            turns = [last if m == 0 else pltpu.roll(last, TAIL * m, 1) for m in range(4)]
            for j in range(4):
                moved = main if j == 0 else pltpu.roll(main, TAIL * j, 1)
                ends = jnp.concatenate([turns[(j - s) % 4] for s in range(SEG_LOCAL)], 0)
                low = jnp.where(lane >= TAIL * j, moved, 0.0)
                high = jnp.where(
                    lane < TAIL * j, moved, jnp.where(lane < TAIL * (j + 1), ends, 0.0)
                )
                for half, x in enumerate((low, high)):
                    tile = slice(LANES * half, LANES * (half + 1))
                    out_ref[f, part, j, :USED, tile] = x.astype(jnp.bfloat16)
                    out_ref[f, part, j, USED:, tile] = fill


def spread(odd, mine, own):
    shape = (LOCAL_BINS, 2, 4, DEPTH, 2 * LANES)
    return pl.pallas_call(
        spread_kernel,
        in_specs=[pl.BlockSpec(memory_space=pltpu.SMEM)]
        + [pl.BlockSpec(memory_space=pltpu.VMEM)] * 2,
        out_specs=[pl.BlockSpec(memory_space=pltpu.VMEM)] * 2,
        out_shape=[
            jax.ShapeDtypeStruct(shape, jnp.bfloat16),
            jax.ShapeDtypeStruct((TM, ROWS, LANES), jnp.bfloat16),
        ],
        compiler_params=pltpu.CompilerParams(vmem_limit_bytes=SCOPE),
        cost_estimate=pl.CostEstimate(flops=70_000_000, bytes_accessed=3_000_000, transcendentals=0),
    )(odd, mine, own)


def turned(block, gather):
    lane = lax.broadcasted_iota(jnp.int32, (TAIL, LOCAL_BINS * LANES), 1) % DEPTH
    whole = lax.dot_general(
        block, gather, (((0,), (0,)), ((), ())), preferred_element_type=jnp.float32
    )
    last = jnp.zeros((TAIL, LOCAL_BINS * LANES), jnp.float32)
    for s in range(SEG_LOCAL):
        moved = whole[TAIL * s : TAIL * (s + 1)]
        moved = pltpu.roll(moved, (16 * s - USED) % (LOCAL_BINS * LANES), 1)
        last = jnp.where((lane >= 16 * s) & (lane < 16 * s + 16), moved, last)
    return jnp.concatenate([whole, last], 0).astype(jnp.bfloat16)


def turn_kernel(valid_ref, near_ref, mine_ref, gather_ref, out_ref, weight_ref):
    column = lax.broadcasted_iota(jnp.int32, (1, 2 * SPAN), 1)
    weight = jnp.zeros((1, 2 * SPAN), jnp.float32)
    for p in range(SLOTS):
        here = (column >= WIDTH * p) & (column < WIDTH * (p + 1))
        weight = jnp.where(here, valid_ref[0, p].astype(jnp.float32), weight)
    weight = weight * (1.0 / math.sqrt(SEG_LOCAL * TM))
    weight_ref[...] = weight
    for n, ref in enumerate((near_ref, mine_ref)):
        for i in range(2):
            block = ref[:, i].reshape(TM * ROWS, LANES)
            for order in range(2):
                out_ref[2 * n + i, order] = turned(block, gather_ref[order])


def turn(valid, near, mine, gather):
    shape = (4, 2, WIDTH, LOCAL_BINS * LANES)
    return pl.pallas_call(
        turn_kernel,
        in_specs=[pl.BlockSpec(memory_space=pltpu.VMEM)] * 4,
        out_specs=[pl.BlockSpec(memory_space=pltpu.VMEM)] * 2,
        out_shape=[
            jax.ShapeDtypeStruct(shape, jnp.bfloat16),
            jax.ShapeDtypeStruct((1, 2 * SPAN), jnp.float32),
        ],
        compiler_params=pltpu.CompilerParams(vmem_limit_bytes=SCOPE),
        cost_estimate=pl.CostEstimate(flops=200_000_000, bytes_accessed=3_000_000, transcendentals=0),
    )(valid, near, mine, gather)


def stack_kernel(
    places_ref, weight_ref, ready_ref, far_ref, edge_ref, gather_ref, right_ref, out_hbm,
    last_ref, out_ref, sems,
):
    places = [places_ref[0, p] for p in range(SLOTS)]
    for n, block in enumerate((far_ref[:, 0], far_ref[:, 1], edge_ref[...])):
        for order in range(2):
            last_ref[n, order] = turned(block.reshape(TM * ROWS, LANES), gather_ref[order])
    weight = weight_ref[...]
    zero = jnp.zeros((DEPTH, LANES), jnp.bfloat16)
    copies = []
    for f in range(LOCAL_BINS):
        tile = slice(LANES * f, LANES * (f + 1))

        def picked(p):
            held = ready_ref[jnp.minimum(places[p], 3), p % 2, :, tile]
            late = last_ref[jnp.maximum(places[p] - 4, 0), p % 2, :, tile]
            return jnp.where(places[p] >= 4, late, held)

        tiles = [
            picked(p) + picked(p + 1) if p + 1 < SLOTS else picked(p) for p in range(0, SLOTS, 2)
        ]
        left = jnp.concatenate(
            [jnp.concatenate(tiles[:2], 1), jnp.concatenate(tiles[2:], 1)], 0
        )
        rows = []
        for j in range(4):
            here = []
            for part in range(2):
                pair = [right_ref[f, part, j, :, :LANES], right_ref[f, part, j, :, LANES:]]
                here += [zero] * j + pair + [zero] * (3 - j)
            rows.append(jnp.concatenate(here, 1))
        products = jnp.dot(left, jnp.concatenate(rows, 0), preferred_element_type=jnp.float32)
        for part in range(2):
            product = products[:, SPAN * part : SPAN * (part + 1)]
            out_ref[part, f, :, :SPAN] = (product[:WIDTH] * weight[:, :SPAN]).astype(jnp.bfloat16)
            out_ref[part, f, :, SPAN:] = (
                product[WIDTH:, : SLOTS * WIDTH - SPAN] * weight[:, SPAN : SLOTS * WIDTH]
            ).astype(jnp.bfloat16)
            copy = pltpu.make_async_copy(
                out_ref.at[part, f], out_hbm.at[part, f], sems.at[part, f]
            )
            copy.start()
            copies.append(copy)
    for copy in copies:
        copy.wait()


def stack(places, weight, ready, far, edge, gather, right):
    whole = pl.BlockSpec(memory_space=pltpu.VMEM)
    shape = (2, LOCAL_BINS, WIDTH, SLOTS * WIDTH)
    return pl.pallas_call(
        stack_kernel,
        in_specs=[whole] * 7,
        out_specs=pl.BlockSpec(memory_space=pltpu.HBM),
        out_shape=jax.ShapeDtypeStruct(shape, jnp.bfloat16),
        scratch_shapes=[
            pltpu.VMEM((3, 2, WIDTH, LOCAL_BINS * LANES), jnp.bfloat16),
            pltpu.VMEM(shape, jnp.bfloat16),
            pltpu.SemaphoreType.DMA((2, LOCAL_BINS)),
        ],
        compiler_params=pltpu.CompilerParams(vmem_limit_bytes=SCOPE),
    )(places, weight, ready, far, edge, gather, right)


def place_of(partner, me, side):
    d = partner - me
    at_even = jnp.where(d == -3, 6, d + 2)
    at_odd = jnp.where(d == 3, 6, jnp.where(d <= -2, d + 7, jnp.where(d <= 0, d + 3, d - 1)))
    return jnp.where(side == 1, at_odd, at_even)


def per_device(records, partner, valid):
    blocks = lax.axis_size("pair") * 2
    chan = ("pair", "side")
    side = lax.axis_index("side")
    table = jnp.asarray(spectra_table(records.shape[2]))
    gather, own = (jnp.asarray(x) for x in gather_tables())

    def fetch(array, even, odd):
        source = {c: c + (odd if c % 2 else even) for c in range(blocks)}
        last = blocks - 1
        if even == 2:
            source[1], source[last - 1] = 0, last
        elif even == 1:
            pass
        elif even == -3:
            source[0], source[2], source[last], source[last - 2] = 2, 0, last - 2, last
        else:
            source[0], source[2] = 1, 0
            source[last], source[last - 2] = last - 1, last
        return lax.ppermute(array, chan, [(f, c) for c, f in source.items()])

    white = whiten(records, table)
    mine = lax.all_to_all(
        white.reshape(2 * TM, ROWS, LANES), ("tm", "side"), 0, 0, tiled=True
    ).reshape(TM, 2, ROWS, LANES)
    near = fetch(mine, -1, 1)
    odd = side.reshape(1)
    right, alone = spread(odd, mine, own)
    edge = fetch(alone, -3, 3)
    far = fetch(near, 1, -1)
    me = lax.axis_index("pair") * 2 + side
    ready, weight = turn(valid, near, mine, gather)
    result = stack(place_of(partner, me, side), weight, ready, far, edge, gather, right)
    return jnp.transpose(result, (0, 1, 3, 2))


def solution(mesh):
    tm, chan = mesh.shape["tm"], mesh.shape["chan"]
    paired = Mesh(mesh.devices.reshape(tm, chan // 2, 2), ("tm", "pair", "side"))
    blocks = ("pair", "side")
    return jax.shard_map(
        per_device,
        mesh=paired,
        in_specs=(P("tm", blocks, None), P(blocks, None), P(blocks, None)),
        out_specs=P(None, "tm", blocks, None),
        check_vma=False,
    )
```
